32 devices in a mesh: row: 16 (over z, y, x), col: 2 (over core).
Axes of the slice: x: 2, y: 2, z: 4, core: 2. Of those that a mesh axis runs over, the one named last changes fastest.
Arguments:
- ham_blocks: bfloat16 [128, 4, 128, 128], P('row'), may hold values from -0.25 to 0.25
- ham_index: int32 [128, 4], P('row'), may hold values from -1 to 127, as said below
- coef_blocks: bfloat16 [8, 16, 128, 128], P('col', 'row'), may hold values from -0.5 to 0.5
- coef_index: int32 [8, 16], P('col', 'row'), may hold values from 0 to 127, as said below
- slab_blocks: bfloat16 [16, 16, 128, 128], P('row', 'col'), may hold values from -0.5 to 0.5
- slab_index: int32 [16, 16], P('row', 'col'), may hold values from 0 to 127, as said below
- pattern_index: int32 [16, 4], P('row', 'col'), may hold values from 0 to 7, as said below
Outputs:
- reduced_blocks: bfloat16 [16, 4, 128, 128], P('row', 'col')
The draws below stay inside these ranges and needn't reach their ends.
Inputs may be any that keep to these rules, and one draw needn't show every extreme that they name: `ham_index`: each row lists its stored block columns first, all distinct, then -1 in every unused slot; a row holds 1 to 4 stored blocks, some row holds 4 and some row only one. `coef_index`: each row names 16 distinct orbital blocks. `slab_index`: each row names 16 distinct orbital blocks. `pattern_index`: entry k of a row names a block among (k // 2) * 4 to (k // 2) * 4 + 3.
All inputs are finite; a program needn't handle non-finite values.
Results may differ from the reference program's by a relative error of at most 0.0049.
Values may be sent and summed in bfloat16 or wider, within the bound.
A program may use at most 128 MiB of HBM per device.

```python
import jax
import jax.numpy as jnp
from jax import lax

BLOCK = 128
HSTORE = 4
CSTORE = 16
OUTSTORE = 2
SFCOL_DEV = 4
PAO_BLOCKS = 128
SF_BLOCKS = 8
SLAB_BLOCKS = 16
OUT_STORED = 4


def distinct_rows(key, row_total, choices_total, picked_total):
    scores = jax.random.randint(key, (row_total, choices_total), 0, 1 << 20) * choices_total
    scores = scores + jnp.arange(choices_total, dtype=jnp.int32)[None, :]
    boost = jnp.zeros((row_total, choices_total), jnp.int32)
    boost = boost.at[0, 0].set(1 << 30).at[0, choices_total - 1].set(1 << 30)
    return lax.top_k(scores + boost, picked_total)[1].astype(jnp.int32)


def draw_ham_index(key, part):
    columns = distinct_rows(jax.random.fold_in(key, 11), PAO_BLOCKS, PAO_BLOCKS, HSTORE)
    counts = jax.random.randint(jax.random.fold_in(key, 12), (PAO_BLOCKS,), 1, HSTORE + 1)
    counts = counts.at[0].set(HSTORE).at[1].set(1)
    keep = jnp.arange(HSTORE, dtype=jnp.int32)[None, :] < counts[:, None]
    return jnp.where(keep, columns, -1).astype(jnp.int32)


def draw_coef_index(key, part):
    return distinct_rows(jax.random.fold_in(key, 13), SF_BLOCKS, PAO_BLOCKS, CSTORE)


def draw_slab_index(key, part):
    return distinct_rows(jax.random.fold_in(key, 14), SLAB_BLOCKS, PAO_BLOCKS, CSTORE)


def draw_pattern_index(key, part):
    groups = jnp.arange(OUT_STORED, dtype=jnp.int32) // OUTSTORE
    within = jax.random.randint(jax.random.fold_in(key, 15), (SLAB_BLOCKS, OUT_STORED), 0, SFCOL_DEV)
    within = within.at[0].set(SFCOL_DEV - 1).at[1].set(0)
    return (groups[None, :] * SFCOL_DEV + within).astype(jnp.int32)


def shard_levels(own_key, dims, pieces, smallest, largest):
    level = 1.0
    for position, parts in pieces:
        heights = jax.random.uniform(jax.random.fold_in(jax.random.fold_in(own_key, 6), position), (parts,), jnp.float32, smallest / len(pieces), largest / len(pieces))
        level = level * jnp.repeat(jnp.exp(heights), dims[position] // parts).reshape((-1,) + (1,) * (len(dims) - 1 - position))
    return level


def noise(stream_key, extent, scale, limit, split=(), kind=jnp.bfloat16):
    values = scale * jax.random.normal(stream_key, extent, jnp.float32)
    if split:
        values = values * shard_levels(stream_key, extent, split, -0.22, 0.18)
    return jnp.clip(values, -limit, limit).astype(kind)


def setup_inputs(seed: int = 0) -> dict:
    seeds = jax.random.split(jax.random.key(seed), 8)
    ham_blocks = noise(seeds[0], (PAO_BLOCKS, HSTORE, BLOCK, BLOCK), (HSTORE * BLOCK) ** -0.5, 0.25, ((0, 16),))
    ham_index = draw_ham_index(jax.random.fold_in(seeds[7], 71), 0)
    coef_blocks = noise(seeds[2], (SF_BLOCKS, CSTORE, BLOCK, BLOCK), BLOCK ** -0.5, 0.5, ((0, 2), (1, 16)))
    coef_index = draw_coef_index(jax.random.fold_in(seeds[7], 71), 0)
    slab_blocks = noise(seeds[4], (SLAB_BLOCKS, CSTORE, BLOCK, BLOCK), BLOCK ** -0.5, 0.5, ((0, 16), (1, 2)))
    slab_index = draw_slab_index(jax.random.fold_in(seeds[7], 71), 0)
    pattern_index = draw_pattern_index(jax.random.fold_in(seeds[7], 71), 0)
    return {"ham_blocks": ham_blocks, "ham_index": ham_index, "coef_blocks": coef_blocks, "coef_index": coef_index, "slab_blocks": slab_blocks, "slab_index": slab_index, "pattern_index": pattern_index}


def reference(ham_blocks, ham_index, coef_blocks, coef_index, slab_blocks, slab_index, pattern_index):
    owners = jnp.broadcast_to(jnp.arange(SF_BLOCKS, dtype=jnp.int32)[:, None], (SF_BLOCKS, CSTORE))
    transposed = jnp.zeros((PAO_BLOCKS, BLOCK, SF_BLOCKS, BLOCK), coef_blocks.dtype)
    transposed = transposed.at[coef_index, :, owners, :].set(jnp.swapaxes(coef_blocks, 2, 3))

    def row_image(row_item):
        block_row, index_row = row_item
        present = (index_row >= 0).astype(jnp.float32)
        gathered = transposed[jnp.maximum(index_row, 0)].astype(jnp.float32)
        masked = block_row.astype(jnp.float32) * present[:, None, None]
        return jnp.einsum("kxb,kbjc->xjc", masked, gathered).astype(jnp.bfloat16)

    images = lax.map(row_image, (ham_blocks, ham_index))

    def slab_row(row_item):
        coef_row, index_row, wanted = row_item
        needed = images[index_row][:, :, wanted, :].astype(jnp.float32)
        summed = jnp.einsum("mab,mbkc->akc", coef_row.astype(jnp.float32), needed)
        return jnp.transpose(summed, (1, 0, 2)).astype(jnp.bfloat16)

    return lax.map(slab_row, (slab_blocks, slab_index, pattern_index))
```

```python
import functools

import jax
import jax.numpy as jnp
from jax import lax
from jax.experimental import pallas as pl
from jax.experimental.pallas import tpu as pltpu
from jax.sharding import PartitionSpec as P

MESH = pl.DeviceIdType.MESH
PLANE = 4


def kernel(dims, pos_ref, where_ref, want_ref, ham_ref, coef_ref, slab_ref, out_ref,
           hbuf, cbuf, sbuf, image, mine, part, got,
           cz_s, cz_r, cp_s, cp_r, cq_s, cq_r, hp_s, hp_r, hq_s, hq_r,
           hc_s, hc_r, sz_s, sz_r, sc_s, sc_r, rz_s, rz_r, loc):
    nrow, ncol, split = dims
    depth = nrow // PLANE
    rows, store = ham_ref.shape[0], ham_ref.shape[1]
    piece = rows // split
    half = piece // 2
    jn, cs = coef_ref.shape[0], coef_ref.shape[1]
    jh = jn // 2
    slots = slab_ref.shape[1]
    wanted = out_ref.shape[1]

    row, col = lax.axis_index("row"), lax.axis_index("col")
    z, g = row // PLANE, lax.rem(row, PLANE)
    xbit, ybit = lax.rem(g, 2), g // 2
    gx = g + 1 - 2 * xbit
    gy = g + 2 - 4 * ybit
    gd = PLANE - 1 - g
    base = z * PLANE
    near = (gx, gy)
    nears = [(base + n, col) for n in near]
    up = lambda t: lax.rem(z + t, depth)
    down = lambda t: lax.rem(z + depth - t, depth)
    line = lambda t: (up(t) * PLANE + g, col)
    peer = lambda t: (row, lax.rem(col + t, ncol))
    source = lambda t: lax.rem(col + ncol - t, ncol)
    part_no = lax.rem(col, split)

    barrier = pltpu.get_barrier_semaphore()
    everyone = nears + [line(t) for t in range(1, depth)] + [peer(t) for t in range(1, ncol)]
    for device in everyone:
        pl.semaphore_signal(barrier, inc=1, device_id=device, device_id_type=MESH)
    pl.semaphore_wait(barrier, len(everyone))

    def copy(src, dst, send, recv, device):
        return pltpu.make_async_remote_copy(
            src_ref=src, dst_ref=dst, send_sem=send, recv_sem=recv, device_id=device, device_id_type=MESH
        )

    def c_line(t, owner):
        return copy(coef_ref, cbuf.at[owner], cz_s.at[t - 1], cz_r.at[t - 1], line(t))

    def c_plane(t, n, a, src, owner):
        return copy(src, cbuf.at[owner, pl.ds(a * jh, jh)], cp_s.at[t, n, a], cp_r.at[t, n, a], nears[n])

    def c_relay(t, n, at):
        ref = cbuf.at[at, pl.ds(n * jh, jh)]
        return copy(ref, ref, cq_s.at[t, n], cq_r.at[t, n], nears[1 - n])

    def h_plane(n, a):
        return copy(ham_ref.at[pl.ds(part_no * piece + a * half, half)],
                    hbuf.at[g, part_no, pl.ds(a * half, half)], hp_s.at[n, a], hp_r.at[n, a], nears[n])

    def h_relay(n):
        ref = hbuf.at[near[n], part_no, pl.ds(n * half, half)]
        return copy(ref, ref, hq_s.at[n], hq_r.at[n], nears[1 - n])

    def h_col(what, t, which):
        ref = hbuf.at[(gx, gy, gd)[what], which]
        return copy(ref, ref, hc_s.at[what, t - 1], hc_r.at[what, t - 1], peer(t))

    def s_line(t, at):
        return copy(slab_ref.at[0], sbuf.at[at, col], sz_s.at[t - 1], sz_r.at[t - 1], line(t))

    def s_col(d, t, at, which):
        ref = sbuf.at[at, which]
        src = slab_ref.at[0] if d == 0 else ref
        return copy(src, ref, sc_s.at[d, t - 1], sc_r.at[d, t - 1], peer(t))

    def r_line(t):
        return copy(part.at[t - 1], got.at[t - 1], rz_s.at[t - 1], rz_r.at[t - 1], line(t))

    sent = []

    def start(c):
        c.start()
        sent.append(c)

    for t in range(1, depth):
        start(c_line(t, row))
    for n in range(2):
        for a in range(2):
            start(c_plane(0, n, a, coef_ref.at[pl.ds(a * jh, jh)], row))
    for n in range(2):
        for a in (n, 1 - n):
            start(h_plane(n, a))
    for t in range(1, ncol):
        start(s_col(0, t, z, col))
    own = [
        pltpu.make_async_copy(coef_ref, cbuf.at[row], loc.at[0]),
        pltpu.make_async_copy(slab_ref.at[0], sbuf.at[z, col], loc.at[1]),
    ]
    own += [
        pltpu.make_async_copy(ham_ref.at[pl.ds(s * piece, piece)], hbuf.at[g, s], loc.at[2 + s])
        for s in range(split)
    ]
    for c in own:
        c.start()
    cbuf[nrow] = jnp.zeros_like(cbuf[nrow])
    image[PLANE * rows] = jnp.zeros_like(image[PLANE * rows])

    for t in range(1, depth):
        at = down(t) * PLANE + g
        c_line(t, at).wait_recv()
        for n in range(2):
            for a in (n, 1 - n):
                start(c_plane(t, n, a, cbuf.at[at, pl.ds(a * jh, jh)], at))
    for t in range(1, depth):
        start(s_line(t, z))
    for t in range(depth):
        for n in range(2):
            at = down(t) * PLANE + near[n]
            c_plane(t, n, n, cbuf.at[at, pl.ds(n * jh, jh)], at).wait_recv()
            start(c_relay(t, n, at))
        if t == 0:
            for n in range(2):
                h_plane(n, n).wait_recv()
                start(h_relay(n))
    for n in range(2):
        h_plane(n, 1 - n).wait_recv()
        if split > 1:
            for t in range(1, ncol):
                start(h_col(n, t, part_no))
    for n in range(2):
        h_relay(n).wait_recv()
    if split > 1:
        for t in range(1, ncol):
            start(h_col(2, t, part_no))
    for t in range(1, depth):
        s_line(t, down(t)).wait_recv()
        for u in range(1, ncol):
            start(s_col(t, u, down(t), col))
    for t in range(depth):
        for n in range(2):
            at = down(t) * PLANE + near[n]
            c_plane(t, n, 1 - n, cbuf.at[at, pl.ds((1 - n) * jh, jh)], at).wait_recv()
        for n in range(2):
            c_relay(t, n, down(t) * PLANE + gd).wait_recv()
    for c in own:
        c.wait()
    if split > 1:
        for what in range(3):
            for t in range(1, ncol):
                h_col(what, t, source(t)).wait_recv()

    def one_row(p, carry):
        owner, line_no = p // rows, lax.rem(p, rows)
        block = hbuf.at[owner, line_no // piece, lax.rem(line_no, piece)]
        lhs = jnp.concatenate([block[k] for k in range(store)], axis=1)
        for j in range(jn):
            picked = []
            for k in range(store):
                slot = pos_ref[(p * store + k) * jn + j]
                picked.append(cbuf[slot // cs, j, lax.rem(slot, cs)] if cs > 1 else cbuf[slot, j, 0])
            rhs = jnp.concatenate(picked, axis=1)
            total = lax.dot_general(lhs, rhs, (((1,), (1,)), ((), ())), preferred_element_type=jnp.float32)
            image[p, j] = total.astype(jnp.bfloat16)
        return carry

    lax.fori_loop(0, PLANE * rows, one_row, 0)

    for d in range(depth):
        for t in range(1, ncol):
            s_col(d, t, down(d), source(t)).wait_recv()

    for t in tuple(range(1, depth)) + (0,):
        at = up(t)
        total = jnp.zeros((out_ref.shape[2], wanted * out_ref.shape[3]), jnp.float32)
        columns = [want_ref[at * wanted + k] for k in range(wanted)]
        for c in range(ncol):
            lhs = jnp.concatenate([sbuf[at, c, m] for m in range(slots)], axis=1)
            rhs = []
            for m in range(slots):
                p = where_ref[(at * ncol + c) * slots + m]
                rhs.append(jnp.concatenate([image[p, j] for j in columns], axis=1))
            total += jnp.dot(lhs, jnp.concatenate(rhs, axis=0), preferred_element_type=jnp.float32)
        for k in range(wanted):
            piece_k = total[:, k * out_ref.shape[3]:(k + 1) * out_ref.shape[3]]
            if t:
                part[t - 1, k] = piece_k.astype(jnp.bfloat16)
            else:
                mine[k] = piece_k
        if t:
            start(r_line(t))
    total = mine[...]
    for t in range(1, depth):
        r_line(t).wait_recv()
        total += got[t - 1].astype(jnp.float32)
    out_ref[0] = total.astype(jnp.bfloat16)
    for c in sent:
        c.wait_send()


def shards(nrow, ncol, ham_blocks, ham_index, coef_blocks, coef_index, slab_blocks, slab_index, pattern_index):
    depth = nrow // PLANE
    rows, store, size = ham_blocks.shape[0], ham_blocks.shape[1], ham_blocks.shape[2]
    jn, cs = coef_blocks.shape[0], coef_blocks.shape[1]
    slots, wanted = slab_blocks.shape[1], pattern_index.shape[1]
    split = ncol if rows % (2 * ncol) == 0 else 1

    row, col = lax.axis_index("row"), lax.axis_index("col")
    z, g = row // PLANE, row % PLANE
    pack = jnp.concatenate([x.reshape(-1) for x in (ham_index, coef_index, slab_index, pattern_index)])
    packs = lax.all_gather(pack, ("row", "col"), axis=0, tiled=False).reshape(depth, PLANE, ncol, -1)
    cuts = [rows * store, jn * cs, slots]
    ends = [sum(cuts[:k + 1]) for k in range(len(cuts))]
    plane = lax.dynamic_index_in_dim(packs, z, 0, keepdims=False)[:, 0, :ends[0]].reshape(-1)
    mine = lax.dynamic_index_in_dim(packs, col, 2, keepdims=False)
    coefs = mine[:, :, ends[0]:ends[1]].reshape(nrow, jn, cs).transpose(1, 0, 2).reshape(jn, nrow * cs)
    match = plane[:, None, None] == coefs[None, :, :]
    number = jnp.arange(nrow * cs, dtype=jnp.int32) - nrow * cs
    pos = nrow * cs + jnp.sum(jnp.where(match, number, 0), axis=2)
    lines = lax.dynamic_index_in_dim(packs, g, 1, keepdims=False)
    where = lines[:, :, ends[1]:ends[2]] - z * PLANE * rows
    where = jnp.where((where >= 0) & (where < PLANE * rows), where, PLANE * rows)
    want = lax.dynamic_index_in_dim(lines, col, 1, keepdims=False)[:, ends[2]:] - col * jn

    smem = pl.BlockSpec(memory_space=pltpu.SMEM)
    vmem = pl.BlockSpec(memory_space=pltpu.VMEM)
    dma = pltpu.SemaphoreType.DMA
    bf16 = jnp.bfloat16
    block = (size, size)
    back = max(depth - 1, 1)
    peers = max(ncol - 1, 1)
    scratch = [
        pltpu.VMEM((PLANE, split, rows // split, store) + block, bf16),
        pltpu.VMEM((nrow + 1, jn, cs) + block, bf16),
        pltpu.VMEM((depth, ncol, slots) + block, bf16),
        pltpu.VMEM((PLANE * rows + 1, jn) + block, bf16),
        pltpu.VMEM((wanted,) + block, jnp.float32),
        pltpu.VMEM((back, wanted) + block, bf16),
        pltpu.VMEM((back, wanted) + block, bf16),
        dma((back,)), dma((back,)),
        dma((depth, 2, 2)), dma((depth, 2, 2)),
        dma((depth, 2)), dma((depth, 2)),
        dma((2, 2)), dma((2, 2)),
        dma((2,)), dma((2,)),
        dma((3, peers)), dma((3, peers)),
        dma((back,)), dma((back,)),
        dma((depth, peers)), dma((depth, peers)),
        dma((back,)), dma((back,)),
        dma((2 + split,)),
    ]
    return pl.pallas_call(
        functools.partial(kernel, (nrow, ncol, split)),
        out_shape=jax.ShapeDtypeStruct((1, wanted) + block, bf16),
        in_specs=[smem] * 3 + [vmem] * 3,
        out_specs=vmem,
        scratch_shapes=scratch,
        compiler_params=pltpu.CompilerParams(
            collective_id=0, has_side_effects=True, vmem_limit_bytes=48 * 1024 * 1024
        ),
    )(pos.reshape(-1), where.reshape(-1), want.reshape(-1), ham_blocks, coef_blocks, slab_blocks)


def solution(mesh):
    placed = (
        P("row", None, None, None),
        P("row", None),
        P("col", "row", None, None),
        P("col", "row"),
        P("row", "col", None, None),
        P("row", "col"),
        P("row", "col"),
    )
    return jax.shard_map(
        functools.partial(shards, mesh.shape["row"], mesh.shape["col"]),
        mesh=mesh, in_specs=placed, out_specs=P("row", "col", None, None), check_vma=False,
    )
```

```python
import functools

import jax
import jax.numpy as jnp
from jax import lax
from jax.experimental import pallas as pl
from jax.experimental.pallas import tpu as pltpu
from jax.sharding import PartitionSpec as P

MESH = pl.DeviceIdType.MESH
PLANE = 4


HEAD = 8


def kernel(dims, pack_ref, ham_ref, coef_ref, slab_ref, out_ref,
           hbuf, cbuf, sbuf, image, mine, part, got, packs, sums, sums_in, table, pos_ref,
           iz_s, iz_r, ip_s, ip_r, ic_s, ic_r,
           cz_s, cz_r, cp_s, cp_r, cq_s, cq_r, hp_s, hp_r, hq_s, hq_r,
           hc_s, hc_r, sz_s, sz_r, sc_s, sc_r, rz_s, rz_r, loc):
    nrow, ncol, split = dims
    depth = nrow // PLANE
    rows, store = ham_ref.shape[0], ham_ref.shape[1]
    piece = rows // split
    half = piece // 2
    jn, cs = coef_ref.shape[0], coef_ref.shape[1]
    jh = jn // 2
    slots = slab_ref.shape[1]
    wanted = out_ref.shape[1]

    row, col = lax.axis_index("row"), lax.axis_index("col")
    z, g = row // PLANE, lax.rem(row, PLANE)
    xbit, ybit = lax.rem(g, 2), g // 2
    gx = g + 1 - 2 * xbit
    gy = g + 2 - 4 * ybit
    gd = PLANE - 1 - g
    base = z * PLANE
    near = (gx, gy)
    nears = [(base + n, col) for n in near]
    up = lambda t: lax.rem(z + t, depth)
    down = lambda t: lax.rem(z + depth - t, depth)
    line = lambda t: (up(t) * PLANE + g, col)
    peer = lambda t: (row, lax.rem(col + t, ncol))
    source = lambda t: lax.rem(col + ncol - t, ncol)
    part_no = lax.rem(col, split)

    barrier = pltpu.get_barrier_semaphore()
    everyone = nears + [(base + gd, col)] + [line(t) for t in range(1, depth)] + [peer(t) for t in range(1, ncol)]
    for device in everyone:
        pl.semaphore_signal(barrier, inc=1, device_id=device, device_id_type=MESH)
    pl.semaphore_wait(barrier, len(everyone))

    def copy(src, dst, send, recv, device):
        return pltpu.make_async_remote_copy(
            src_ref=src, dst_ref=dst, send_sem=send, recv_sem=recv, device_id=device, device_id_type=MESH
        )

    def c_line(t, owner):
        return copy(coef_ref, cbuf.at[owner], cz_s.at[t - 1], cz_r.at[t - 1], line(t))

    def c_plane(t, n, a, src, owner):
        return copy(src, cbuf.at[owner, pl.ds(a * jh, jh)], cp_s.at[t, n, a], cp_r.at[t, n, a], nears[n])

    def c_relay(t, n, at):
        ref = cbuf.at[at, pl.ds(n * jh, jh)]
        return copy(ref, ref, cq_s.at[t, n], cq_r.at[t, n], nears[1 - n])

    def h_plane(n, a):
        return copy(ham_ref.at[pl.ds(part_no * piece + a * half, half)],
                    hbuf.at[g, part_no, pl.ds(a * half, half)], hp_s.at[n, a], hp_r.at[n, a], nears[n])

    def h_relay(n):
        ref = hbuf.at[near[n], part_no, pl.ds(n * half, half)]
        return copy(ref, ref, hq_s.at[n], hq_r.at[n], nears[1 - n])

    def h_col(what, t, which):
        ref = hbuf.at[(gx, gy, gd)[what], which]
        return copy(ref, ref, hc_s.at[what, t - 1], hc_r.at[what, t - 1], peer(t))

    def s_line(t, at):
        return copy(slab_ref.at[0], sbuf.at[at, col], sz_s.at[t - 1], sz_r.at[t - 1], line(t))

    def s_col(d, t, at, which):
        ref = sbuf.at[at, which]
        src = slab_ref.at[0] if d == 0 else ref
        return copy(src, ref, sc_s.at[d, t - 1], sc_r.at[d, t - 1], peer(t))

    def r_line(t):
        return copy(part.at[t - 1], got.at[t - 1], rz_s.at[t - 1], rz_r.at[t - 1], line(t))

    def i_line(t, at):
        return copy(pack_ref, packs.at[g, at], iz_s.at[t - 1], iz_r.at[t - 1], line(t))

    def i_plane(n, owner):
        device = (base + (gx, gy, gd)[n], col)
        return copy(packs.at[owner], packs.at[owner], ip_s.at[n], ip_r.at[n], device)

    def i_col(t):
        return copy(sums, sums_in.at[t - 1], ic_s.at[t - 1], ic_r.at[t - 1], peer(t))

    sent = []

    def start(c):
        c.start()
        sent.append(c)

    for t in range(1, depth):
        start(i_line(t, z))
    for t in range(1, depth):
        start(c_line(t, row))
    for n in range(2):
        for a in range(2):
            start(c_plane(0, n, a, coef_ref.at[pl.ds(a * jh, jh)], row))
    for t in range(1, ncol):
        start(s_col(0, t, z, col))
    own = [
        pltpu.make_async_copy(coef_ref, cbuf.at[row], loc.at[0]),
        pltpu.make_async_copy(slab_ref.at[0], sbuf.at[z, col], loc.at[1]),
    ]
    own += [
        pltpu.make_async_copy(ham_ref.at[pl.ds(s * piece, piece)], hbuf.at[g, s], loc.at[2 + s])
        for s in range(split)
    ]
    for c in own:
        c.start()
    cbuf[nrow] = jnp.zeros_like(cbuf[nrow])
    image[PLANE * rows] = jnp.zeros_like(image[PLANE * rows])

    packs[g, z] = pack_ref[...]
    for t in range(1, depth):
        i_line(t, down(t)).wait_recv()
    for n in range(3):
        start(i_plane(n, g))
    total = packs[g, 0, :HEAD]
    for t in range(1, depth):
        total += packs[g, t, :HEAD]
    sums[...] = total
    for t in range(1, ncol):
        start(i_col(t))

    for t in range(1, depth):
        at = down(t) * PLANE + g
        c_line(t, at).wait_recv()
        for n in range(2):
            for a in (n, 1 - n):
                start(c_plane(t, n, a, cbuf.at[at, pl.ds(a * jh, jh)], at))
        if t == max(depth - 2, 1):
            for n in range(2):
                start(h_plane(n, n))
    for n in range(2):
        start(h_plane(n, 1 - n))
    for t in range(1, depth):
        start(s_line(t, z))

    for n in range(3):
        i_plane(n, (gx, gy, gd)[n]).wait_recv()
    for t in range(1, ncol):
        i_col(t).wait_recv()
    lanes = table.shape[1]
    wanted_q = packs[0, z, 0:1]
    for n in range(1, PLANE):
        wanted_q += packs[n, z, 0:1]
    wanted_q = jnp.broadcast_to(wanted_q, (jn, lanes))
    pos = jnp.full((jn, lanes), nrow * cs, jnp.int32)
    for r in range(nrow):
        for s in range(cs):
            named = packs[r % PLANE, r // PLANE, HEAD + s * jn:HEAD + (s + 1) * jn]
            pos = jnp.where(wanted_q == named, r * cs + s, pos)
    table[...] = jnp.zeros_like(table)
    table[0:jn] = pos
    both = sums[...]
    for t in range(1, ncol):
        both += sums_in[t - 1]
    where = both[1:2] - base * rows
    table[jn:jn + 1] = jnp.where((where >= 0) & (where < PLANE * rows), where, PLANE * rows)
    table[jn + 1:jn + 2] = jnp.minimum(jnp.maximum(both[2:3] - col * jn, 0), jn - 1)
    to_scalars = pltpu.make_async_copy(table, pos_ref, loc.at[2 + split])
    to_scalars.start()

    for t in range(depth):
        for n in range(2):
            at = down(t) * PLANE + near[n]
            c_plane(t, n, n, cbuf.at[at, pl.ds(n * jh, jh)], at).wait_recv()
            start(c_relay(t, n, at))
    for t in range(depth):
        for n in range(2):
            at = down(t) * PLANE + near[n]
            c_plane(t, n, 1 - n, cbuf.at[at, pl.ds((1 - n) * jh, jh)], at).wait_recv()
    for n in range(2):
        h_plane(n, n).wait_recv()
        start(h_relay(n))
    for t in range(depth):
        for n in range(2):
            c_relay(t, n, down(t) * PLANE + gd).wait_recv()
    for c in own:
        c.wait()
    to_scalars.wait()

    def rows_of(owner, first, count):
        def one_row(i, carry):
            line_no = first + i
            block = hbuf.at[owner, line_no // piece, lax.rem(line_no, piece)]
            p = owner * rows + line_no
            lhs = jnp.concatenate([block[k] for k in range(store)], axis=1)
            picks = []
            for j in range(jn):
                picked = []
                for k in range(store):
                    slot = pos_ref[j, p * store + k]
                    picked.append(cbuf[slot // cs, j, lax.rem(slot, cs)] if cs > 1 else cbuf[slot, j, 0])
                picks.append(jnp.concatenate(picked, axis=1))
            rhs = jnp.concatenate(picks, axis=0)
            total = lax.dot_general(lhs, rhs, (((1,), (1,)), ((), ())), preferred_element_type=jnp.float32)
            for j in range(jn):
                width = total.shape[1] // jn
                image[p, j] = total[:, j * width:(j + 1) * width].astype(jnp.bfloat16)
            return carry

        lax.fori_loop(0, count, one_row, 0)

    rows_of(g, 0, rows)
    for n in range(2):
        h_plane(n, 1 - n).wait_recv()
        if split > 1:
            for t in range(1, ncol):
                start(h_col(n, t, part_no))
    for t in range(1, depth):
        s_line(t, down(t)).wait_recv()
        for u in range(1, ncol):
            start(s_col(t, u, down(t), col))
        if t == 1:
            for n in range(2):
                rows_of(near[n], part_no * piece, piece)
            for n in range(2):
                h_relay(n).wait_recv()
            if split > 1:
                for u in range(1, ncol):
                    start(h_col(2, u, part_no))
            rows_of(gd, part_no * piece, piece)
    if split > 1:
        for what in range(3):
            for t in range(1, ncol):
                h_col(what, t, source(t)).wait_recv()
                rows_of((gx, gy, gd)[what], source(t) * piece, piece)

    for d in range(depth):
        for t in range(1, ncol):
            s_col(d, t, down(d), source(t)).wait_recv()

    for t in tuple(range(1, depth)) + (0,):
        at = up(t)
        total = jnp.zeros((out_ref.shape[2], wanted * out_ref.shape[3]), jnp.float32)
        columns = [pos_ref[jn + 1, (col * depth + at) * wanted + k] for k in range(wanted)]
        for c in range(ncol):
            lhs = jnp.concatenate([sbuf[at, c, m] for m in range(slots)], axis=1)
            rhs = []
            for m in range(slots):
                p = pos_ref[jn, (at * ncol + c) * slots + m]
                rhs.append(jnp.concatenate([image[p, j] for j in columns], axis=1))
            total += jnp.dot(lhs, jnp.concatenate(rhs, axis=0), preferred_element_type=jnp.float32)
        for k in range(wanted):
            piece_k = total[:, k * out_ref.shape[3]:(k + 1) * out_ref.shape[3]]
            if t:
                part[t - 1, k] = piece_k.astype(jnp.bfloat16)
            else:
                mine[k] = piece_k
        if t:
            start(r_line(t))
    total = mine[...]
    for t in range(1, depth):
        r_line(t).wait_recv()
        total += got[t - 1].astype(jnp.float32)
    out_ref[0] = total.astype(jnp.bfloat16)
    for c in sent:
        c.wait_send()


def shards(nrow, ncol, ham_blocks, ham_index, coef_blocks, coef_index, slab_blocks, slab_index, pattern_index):
    depth = nrow // PLANE
    rows, store, size = ham_blocks.shape[0], ham_blocks.shape[1], ham_blocks.shape[2]
    jn, cs = coef_blocks.shape[0], coef_blocks.shape[1]
    slots, wanted = slab_blocks.shape[1], pattern_index.shape[1]
    split = ncol if rows % (2 * ncol) == 0 else 1

    row, col = lax.axis_index("row"), lax.axis_index("col")
    z, g = row // PLANE, row % PLANE
    lanes = max(PLANE * rows * store, depth * ncol * max(slots, wanted))
    lanes += -lanes % 128
    lane = jnp.arange(lanes, dtype=jnp.int32)

    def spread(values, at):
        flat = values.reshape(-1)
        copies = jnp.tile(flat, -(-lanes // flat.size))[:lanes]
        return jnp.where(lane // flat.size == at, copies, 0)[None]

    named = jnp.broadcast_to(coef_index.T.reshape(-1)[:, None], (jn * cs, lanes))
    pack = jnp.concatenate([
        spread(ham_index, g),
        spread(slab_index, z * ncol + col),
        spread(pattern_index, col * depth + z),
        jnp.zeros((HEAD - 3, lanes), jnp.int32),
        named,
        jnp.zeros((-(jn * cs) % 8, lanes), jnp.int32),
    ])
    height = pack.shape[0]

    vmem = pl.BlockSpec(memory_space=pltpu.VMEM)
    dma = pltpu.SemaphoreType.DMA
    bf16 = jnp.bfloat16
    block = (size, size)
    back = max(depth - 1, 1)
    peers = max(ncol - 1, 1)
    tall = jn + 2 + -(jn + 2) % 8
    scratch = [
        pltpu.VMEM((PLANE, split, rows // split, store) + block, bf16),
        pltpu.VMEM((nrow + 1, jn, cs) + block, bf16),
        pltpu.VMEM((depth, ncol, slots) + block, bf16),
        pltpu.VMEM((PLANE * rows + 1, jn) + block, bf16),
        pltpu.VMEM((wanted,) + block, jnp.float32),
        pltpu.VMEM((back, wanted) + block, bf16),
        pltpu.VMEM((back, wanted) + block, bf16),
        pltpu.VMEM((PLANE, depth, height, lanes), jnp.int32),
        pltpu.VMEM((HEAD, lanes), jnp.int32),
        pltpu.VMEM((peers, HEAD, lanes), jnp.int32),
        pltpu.VMEM((tall, lanes), jnp.int32),
        pltpu.SMEM((tall, lanes), jnp.int32),
        dma((back,)), dma((back,)),
        dma((3,)), dma((3,)),
        dma((peers,)), dma((peers,)),
        dma((back,)), dma((back,)),
        dma((depth, 2, 2)), dma((depth, 2, 2)),
        dma((depth, 2)), dma((depth, 2)),
        dma((2, 2)), dma((2, 2)),
        dma((2,)), dma((2,)),
        dma((3, peers)), dma((3, peers)),
        dma((back,)), dma((back,)),
        dma((depth, peers)), dma((depth, peers)),
        dma((back,)), dma((back,)),
        dma((3 + split,)),
    ]
    return pl.pallas_call(
        functools.partial(kernel, (nrow, ncol, split)),
        out_shape=jax.ShapeDtypeStruct((1, wanted) + block, bf16),
        in_specs=[vmem] * 4,
        out_specs=vmem,
        scratch_shapes=scratch,
        compiler_params=pltpu.CompilerParams(
            collective_id=0, has_side_effects=True, vmem_limit_bytes=48 * 1024 * 1024
        ),
    )(pack, ham_blocks, coef_blocks, slab_blocks)


def solution(mesh):
    placed = (
        P("row", None, None, None),
        P("row", None),
        P("col", "row", None, None),
        P("col", "row"),
        P("row", "col", None, None),
        P("row", "col"),
        P("row", "col"),
    )
    return jax.shard_map(
        functools.partial(shards, mesh.shape["row"], mesh.shape["col"]),
        mesh=mesh, in_specs=placed, out_specs=P("row", "col", None, None), check_vma=False,
    )
```

```python
import functools

import jax
import jax.numpy as jnp
from jax import lax
from jax.experimental import pallas as pl
from jax.experimental.pallas import tpu as pltpu
from jax.sharding import PartitionSpec as P

MESH = pl.DeviceIdType.MESH
PLANE = 4


HEAD = 8


def kernel(dims, pack_ref, ham_ref, coef_ref, slab_ref, out_ref,
           hbuf, cbuf, sbuf, image, mine, part, got, packs, sums, sums_in, table, pos_ref,
           iz_s, iz_r, ip_s, ip_r, ic_s, ic_r,
           cz_s, cz_r, cp_s, cp_r, cq_s, cq_r, hp_s, hp_r, hq_s, hq_r,
           hc_s, hc_r, sz_s, sz_r, sc_s, sc_r, rz_s, rz_r, loc):
    nrow, ncol, split = dims
    depth = nrow // PLANE
    rows, store = ham_ref.shape[0], ham_ref.shape[1]
    piece = rows // split
    half = piece // 2
    jn, cs = coef_ref.shape[0], coef_ref.shape[1]
    jh = jn // 2
    slots = slab_ref.shape[1]
    wanted = out_ref.shape[1]

    row, col = lax.axis_index("row"), lax.axis_index("col")
    z, g = row // PLANE, lax.rem(row, PLANE)
    xbit, ybit = lax.rem(g, 2), g // 2
    gx = g + 1 - 2 * xbit
    gy = g + 2 - 4 * ybit
    gd = PLANE - 1 - g
    base = z * PLANE
    near = (gx, gy)
    nears = [(base + n, col) for n in near]
    up = lambda t: lax.rem(z + t, depth)
    down = lambda t: lax.rem(z + depth - t, depth)
    line = lambda t: (up(t) * PLANE + g, col)
    peer = lambda t: (row, lax.rem(col + t, ncol))
    source = lambda t: lax.rem(col + ncol - t, ncol)
    part_no = lax.rem(col, split)

    barrier = pltpu.get_barrier_semaphore()
    everyone = nears + [(base + gd, col)] + [line(t) for t in range(1, depth)] + [peer(t) for t in range(1, ncol)]
    for device in everyone:
        pl.semaphore_signal(barrier, inc=1, device_id=device, device_id_type=MESH)
    pl.semaphore_wait(barrier, len(everyone))

    def copy(src, dst, send, recv, device):
        return pltpu.make_async_remote_copy(
            src_ref=src, dst_ref=dst, send_sem=send, recv_sem=recv, device_id=device, device_id_type=MESH
        )

    def c_line(t, owner):
        return copy(coef_ref, cbuf.at[owner], cz_s.at[t - 1], cz_r.at[t - 1], line(t))

    def c_plane(t, n, a, src, owner):
        return copy(src, cbuf.at[owner, pl.ds(a * jh, jh)], cp_s.at[t, n, a], cp_r.at[t, n, a], nears[n])

    def c_relay(t, n, at):
        ref = cbuf.at[at, pl.ds(n * jh, jh)]
        return copy(ref, ref, cq_s.at[t, n], cq_r.at[t, n], nears[1 - n])

    def h_plane(n, a):
        return copy(ham_ref.at[pl.ds(part_no * piece + a * half, half)],
                    hbuf.at[g, part_no, pl.ds(a * half, half)], hp_s.at[n, a], hp_r.at[n, a], nears[n])

    def h_relay(n):
        ref = hbuf.at[near[n], part_no, pl.ds(n * half, half)]
        return copy(ref, ref, hq_s.at[n], hq_r.at[n], nears[1 - n])

    def h_col(what, t, which):
        ref = hbuf.at[(gx, gy, gd)[what], which]
        return copy(ref, ref, hc_s.at[what, t - 1], hc_r.at[what, t - 1], peer(t))

    def s_line(t, at):
        return copy(slab_ref.at[0], sbuf.at[at, col], sz_s.at[t - 1], sz_r.at[t - 1], line(t))

    def s_col(d, t, at, which):
        ref = sbuf.at[at, which]
        src = slab_ref.at[0] if d == 0 else ref
        return copy(src, ref, sc_s.at[d, t - 1], sc_r.at[d, t - 1], peer(t))

    def r_line(t):
        return copy(part.at[t - 1], got.at[t - 1], rz_s.at[t - 1], rz_r.at[t - 1], line(t))

    def i_line(t, at):
        return copy(pack_ref, packs.at[g, at], iz_s.at[t - 1], iz_r.at[t - 1], line(t))

    def i_plane(n, owner):
        device = (base + (gx, gy, gd)[n], col)
        return copy(packs.at[owner], packs.at[owner], ip_s.at[n], ip_r.at[n], device)

    def i_col(t):
        return copy(sums, sums_in.at[t - 1], ic_s.at[t - 1], ic_r.at[t - 1], peer(t))

    sent = []

    def start(c):
        c.start()
        sent.append(c)

    for t in range(1, depth):
        start(i_line(t, z))
    for t in range(1, depth):
        start(c_line(t, row))
    for n in range(2):
        for a in range(2):
            start(c_plane(0, n, a, coef_ref.at[pl.ds(a * jh, jh)], row))
    for n in range(2):
        start(h_plane(n, n))
        start(h_plane(n, 1 - n))
    for t in range(1, ncol):
        start(s_col(0, t, z, col))
    own = [
        pltpu.make_async_copy(coef_ref, cbuf.at[row], loc.at[0]),
        pltpu.make_async_copy(slab_ref.at[0], sbuf.at[z, col], loc.at[1]),
    ]
    own += [
        pltpu.make_async_copy(ham_ref.at[pl.ds(s * piece, piece)], hbuf.at[g, s], loc.at[2 + s])
        for s in range(split)
    ]
    for c in own:
        c.start()
    cbuf[nrow] = jnp.zeros_like(cbuf[nrow])
    image[PLANE * rows] = jnp.zeros_like(image[PLANE * rows])

    packs[g, z] = pack_ref[...]
    for t in range(1, depth):
        i_line(t, down(t)).wait_recv()
    for n in range(3):
        start(i_plane(n, g))
    total = packs[g, 0, :HEAD]
    for t in range(1, depth):
        total += packs[g, t, :HEAD]
    sums[...] = total
    for t in range(1, ncol):
        start(i_col(t))

    for t in range(1, depth):
        at = down(t) * PLANE + g
        c_line(t, at).wait_recv()
        for n in range(2):
            for a in (n, 1 - n):
                start(c_plane(t, n, a, cbuf.at[at, pl.ds(a * jh, jh)], at))
    for t in range(1, depth):
        start(s_line(t, z))

    for n in range(3):
        i_plane(n, (gx, gy, gd)[n]).wait_recv()
    for t in range(1, ncol):
        i_col(t).wait_recv()
    lanes = table.shape[1]
    wanted_q = packs[0, z, 0:1]
    for n in range(1, PLANE):
        wanted_q += packs[n, z, 0:1]
    wanted_q = jnp.broadcast_to(wanted_q, (jn, lanes))
    pos = jnp.full((jn, lanes), nrow * cs, jnp.int32)
    for r in range(nrow):
        for s in range(cs):
            named = packs[r % PLANE, r // PLANE, HEAD + s * jn:HEAD + (s + 1) * jn]
            pos = jnp.where(wanted_q == named, r * cs + s, pos)
    table[...] = jnp.zeros_like(table)
    table[0:jn] = pos
    both = sums[...]
    for t in range(1, ncol):
        both += sums_in[t - 1]
    where = both[1:2] - base * rows
    table[jn:jn + 1] = jnp.where((where >= 0) & (where < PLANE * rows), where, PLANE * rows)
    table[jn + 1:jn + 2] = jnp.minimum(jnp.maximum(both[2:3] - col * jn, 0), jn - 1)
    to_scalars = pltpu.make_async_copy(table, pos_ref, loc.at[2 + split])
    to_scalars.start()

    for t in range(depth):
        for n in range(2):
            at = down(t) * PLANE + near[n]
            c_plane(t, n, n, cbuf.at[at, pl.ds(n * jh, jh)], at).wait_recv()
            start(c_relay(t, n, at))
    for t in range(depth):
        for n in range(2):
            at = down(t) * PLANE + near[n]
            c_plane(t, n, 1 - n, cbuf.at[at, pl.ds((1 - n) * jh, jh)], at).wait_recv()
    for n in range(2):
        h_plane(n, n).wait_recv()
        start(h_relay(n))
    for t in range(depth):
        for n in range(2):
            c_relay(t, n, down(t) * PLANE + gd).wait_recv()
    for c in own:
        c.wait()
    to_scalars.wait()

    def rows_of(owner, first, count):
        def one_row(i, carry):
            line_no = first + i
            block = hbuf.at[owner, line_no // piece, lax.rem(line_no, piece)]
            p = owner * rows + line_no
            lhs = jnp.concatenate([block[k] for k in range(store)], axis=1)
            picks = []
            for j in range(jn):
                picked = []
                for k in range(store):
                    slot = pos_ref[j, p * store + k]
                    picked.append(cbuf[slot // cs, j, lax.rem(slot, cs)] if cs > 1 else cbuf[slot, j, 0])
                picks.append(jnp.concatenate(picked, axis=1))
            rhs = jnp.concatenate(picks, axis=0)
            total = lax.dot_general(lhs, rhs, (((1,), (1,)), ((), ())), preferred_element_type=jnp.float32)
            for j in range(jn):
                width = total.shape[1] // jn
                image[p, j] = total[:, j * width:(j + 1) * width].astype(jnp.bfloat16)
            return carry

        lax.fori_loop(0, count, one_row, 0)

    rows_of(g, 0, rows)
    for n in range(2):
        h_plane(n, 1 - n).wait_recv()
        if split > 1:
            for t in range(1, ncol):
                start(h_col(n, t, part_no))
    for t in range(1, depth):
        s_line(t, down(t)).wait_recv()
        for u in range(1, ncol):
            start(s_col(t, u, down(t), col))
        if t == 1:
            for n in range(2):
                rows_of(near[n], part_no * piece, piece)
            for n in range(2):
                h_relay(n).wait_recv()
            if split > 1:
                for u in range(1, ncol):
                    start(h_col(2, u, part_no))
            rows_of(gd, part_no * piece, piece)
    if split > 1:
        for what in range(3):
            for t in range(1, ncol):
                h_col(what, t, source(t)).wait_recv()
                rows_of((gx, gy, gd)[what], source(t) * piece, piece)

    for d in range(depth):
        for t in range(1, ncol):
            s_col(d, t, down(d), source(t)).wait_recv()

    for t in tuple(range(1, depth)) + (0,):
        at = up(t)
        total = jnp.zeros((out_ref.shape[2], wanted * out_ref.shape[3]), jnp.float32)
        columns = [pos_ref[jn + 1, (col * depth + at) * wanted + k] for k in range(wanted)]
        for c in range(ncol):
            lhs = jnp.concatenate([sbuf[at, c, m] for m in range(slots)], axis=1)
            rhs = []
            for m in range(slots):
                p = pos_ref[jn, (at * ncol + c) * slots + m]
                rhs.append(jnp.concatenate([image[p, j] for j in columns], axis=1))
            total += jnp.dot(lhs, jnp.concatenate(rhs, axis=0), preferred_element_type=jnp.float32)
        for k in range(wanted):
            piece_k = total[:, k * out_ref.shape[3]:(k + 1) * out_ref.shape[3]]
            if t:
                part[t - 1, k] = piece_k.astype(jnp.bfloat16)
            else:
                mine[k] = piece_k
        if t:
            start(r_line(t))
    total = mine[...]
    for t in range(1, depth):
        r_line(t).wait_recv()
        total += got[t - 1].astype(jnp.float32)
    out_ref[0] = total.astype(jnp.bfloat16)
    for c in sent:
        c.wait_send()


def shards(nrow, ncol, ham_blocks, ham_index, coef_blocks, coef_index, slab_blocks, slab_index, pattern_index):
    depth = nrow // PLANE
    rows, store, size = ham_blocks.shape[0], ham_blocks.shape[1], ham_blocks.shape[2]
    jn, cs = coef_blocks.shape[0], coef_blocks.shape[1]
    slots, wanted = slab_blocks.shape[1], pattern_index.shape[1]
    split = ncol if rows % (2 * ncol) == 0 else 1

    row, col = lax.axis_index("row"), lax.axis_index("col")
    z, g = row // PLANE, row % PLANE
    lanes = max(PLANE * rows * store, depth * ncol * max(slots, wanted))
    lanes += -lanes % 128
    lane = jnp.arange(lanes, dtype=jnp.int32)

    def spread(values, at):
        flat = values.reshape(-1)
        copies = jnp.tile(flat, -(-lanes // flat.size))[:lanes]
        return jnp.where(lane // flat.size == at, copies, 0)[None]

    named = jnp.broadcast_to(coef_index.T.reshape(-1)[:, None], (jn * cs, lanes))
    pack = jnp.concatenate([
        spread(ham_index, g),
        spread(slab_index, z * ncol + col),
        spread(pattern_index, col * depth + z),
        jnp.zeros((HEAD - 3, lanes), jnp.int32),
        named,
        jnp.zeros((-(jn * cs) % 8, lanes), jnp.int32),
    ])
    height = pack.shape[0]

    vmem = pl.BlockSpec(memory_space=pltpu.VMEM)
    dma = pltpu.SemaphoreType.DMA
    bf16 = jnp.bfloat16
    block = (size, size)
    back = max(depth - 1, 1)
    peers = max(ncol - 1, 1)
    tall = jn + 2 + -(jn + 2) % 8
    scratch = [
        pltpu.VMEM((PLANE, split, rows // split, store) + block, bf16),
        pltpu.VMEM((nrow + 1, jn, cs) + block, bf16),
        pltpu.VMEM((depth, ncol, slots) + block, bf16),
        pltpu.VMEM((PLANE * rows + 1, jn) + block, bf16),
        pltpu.VMEM((wanted,) + block, jnp.float32),
        pltpu.VMEM((back, wanted) + block, bf16),
        pltpu.VMEM((back, wanted) + block, bf16),
        pltpu.VMEM((PLANE, depth, height, lanes), jnp.int32),
        pltpu.VMEM((HEAD, lanes), jnp.int32),
        pltpu.VMEM((peers, HEAD, lanes), jnp.int32),
        pltpu.VMEM((tall, lanes), jnp.int32),
        pltpu.SMEM((tall, lanes), jnp.int32),
        dma((back,)), dma((back,)),
        dma((3,)), dma((3,)),
        dma((peers,)), dma((peers,)),
        dma((back,)), dma((back,)),
        dma((depth, 2, 2)), dma((depth, 2, 2)),
        dma((depth, 2)), dma((depth, 2)),
        dma((2, 2)), dma((2, 2)),
        dma((2,)), dma((2,)),
        dma((3, peers)), dma((3, peers)),
        dma((back,)), dma((back,)),
        dma((depth, peers)), dma((depth, peers)),
        dma((back,)), dma((back,)),
        dma((3 + split,)),
    ]
    return pl.pallas_call(
        functools.partial(kernel, (nrow, ncol, split)),
        out_shape=jax.ShapeDtypeStruct((1, wanted) + block, bf16),
        in_specs=[vmem] * 4,
        out_specs=vmem,
        scratch_shapes=scratch,
        compiler_params=pltpu.CompilerParams(
            collective_id=0, has_side_effects=True, vmem_limit_bytes=48 * 1024 * 1024
        ),
    )(pack, ham_blocks, coef_blocks, slab_blocks)


def solution(mesh):
    placed = (
        P("row", None, None, None),
        P("row", None),
        P("col", "row", None, None),
        P("col", "row"),
        P("row", "col", None, None),
        P("row", "col"),
        P("row", "col"),
    )
    return jax.shard_map(
        functools.partial(shards, mesh.shape["row"], mesh.shape["col"]),
        mesh=mesh, in_specs=placed, out_specs=P("row", "col", None, None), check_vma=False,
    )
```
